256 devices in a mesh: ty: 16 (over z, core), tx: 16 (over x, y).
Axes of the slice: x: 4, y: 4, z: 8, core: 2. Of those that a mesh axis runs over, the one named last changes fastest.
Arguments:
- object_planes: float32 [2, 2, 4096, 4096], P(None, None, 'ty', 'tx'), may hold values from -5 to 5
- probe: float32 [2, 256, 256], replicated, may hold values from -6 to 6
- positions: int32 [16, 16, 2, 2], P('ty', 'tx'), may hold values from 0 to 255
- measured: float32 [16, 16, 2, 256, 256], P('ty', 'tx'), may hold values from 0.2 to 3
Outputs:
- new_object: float32 [2, 2, 4096, 4096], P(None, None, 'ty', 'tx')
- new_probe: float32 [2, 256, 256], replicated
The draws below stay inside these ranges and needn't reach their ends.
All inputs are finite; a program needn't handle non-finite values.
Results may differ from the reference program's by a relative error of at most 0.00019.
Values sent between devices are 32-bit elements; how exact they have to be, the bound alone decides.
A program may use at most 128 MiB of HBM per device.

```python
import math
import jax
import jax.numpy as jnp
from jax import lax

PATCH_WIDTH = 256
TILE = 256
SLICES = 2
ITERS = 2
P_DEV = 2
OBJ_R = 4096
OBJ_C = 4096
N_TY = 16
N_TX = 16


def set_ends(result, stream_key, smallest, largest):
    dims = result.shape
    index_at = [jax.random.randint(jax.random.fold_in(stream_key, axis), (), 0, dims[axis]) for axis in range(len(dims))]
    result = result.at[tuple(index_at)].set(smallest)
    longest = dims.index(max(dims))
    index_at[longest] = (index_at[longest] + 1) % dims[longest]
    return result.at[tuple(index_at)].set(largest)


def block_levels(own_key, dims, pieces, smallest, top_value):
    def one(axis_at, shards_of):
        heights = jax.random.uniform(jax.random.fold_in(jax.random.fold_in(own_key, 6), axis_at), (shards_of,), jnp.float32, smallest / len(pieces), top_value / len(pieces))
        return jnp.repeat(jnp.exp(heights), dims[axis_at] // shards_of).reshape((-1,) + (1,) * (len(dims) - axis_at - 1))

    level = one(*pieces[0])
    for cut in pieces[1:]:
        level = level * one(*cut)
    return level


def normal_values(own_key, extent, scale, bound, cuts=(), kind=jnp.bfloat16):
    array = scale * jax.random.normal(own_key, extent, jnp.float32)
    if cuts:
        array = array * block_levels(own_key, extent, cuts, -0.22, 0.18)
    return jnp.clip(array, -bound, bound).astype(kind)


def setup_inputs(seed: int = 0) -> dict:
    key_of = jax.random.split(jax.random.key(seed), 5)
    return {
        "object_planes": normal_values(key_of[0], (SLICES, 2, OBJ_R, OBJ_C), 0.7, 5.0, ((2, 16), (3, 16)), jnp.float32),
        "probe": normal_values(key_of[1], (2, PATCH_WIDTH, PATCH_WIDTH), 1.0, 6.0, (), jnp.float32),
        "positions": set_ends(jax.random.randint(key_of[2], (N_TY, N_TX, P_DEV, 2), 0, TILE), jax.random.fold_in(key_of[2], 1), 0, TILE - 1).astype(jnp.int32),
        "measured": jnp.clip(0.2 + 2.8 * jax.random.uniform(key_of[3], (N_TY, N_TX, P_DEV, PATCH_WIDTH, PATCH_WIDTH), jnp.float32) ** block_levels(key_of[3], (N_TY, N_TX, P_DEV, PATCH_WIDTH, PATCH_WIDTH), ((0, 16), (1, 16)), -0.2, 0.2), 0.2, 3.0),
    }


def fresnel_kernel(size):
    index = jnp.arange(size, dtype=jnp.int32)
    quad = (index[:, None] * index[:, None] + index[None, :] * index[None, :]) % (2 * size)
    phase = -math.pi * quad.astype(jnp.float32) / size
    return (jnp.cos(phase), jnp.sin(phase))

def single_patch_loss(object_patch, probe, measured_intensity):
    kernel_re, kernel_im = fresnel_kernel(PATCH_WIDTH)
    kernel = kernel_re + 1j * kernel_im
    field = (probe[0] + 1j * probe[1]) * (object_patch[0, 0] + 1j * object_patch[0, 1])
    for s in range(1, SLICES):
        spectrum = jnp.fft.fft2(field, norm='ortho') * kernel
        field = jnp.fft.ifft2(spectrum, norm='ortho') * (object_patch[s, 0] + 1j * object_patch[s, 1])
    far = jnp.fft.fft2(field, norm='ortho')
    model_amplitude = jnp.sqrt(jnp.real(far) ** 2 + jnp.imag(far) ** 2 + 1.0)
    return 0.5 * jnp.sum((model_amplitude - measured_intensity) ** 2)

def reference(object_planes, probe, positions, measured):
    scan_rows = (jnp.arange(N_TY, dtype=jnp.int32)[:, None, None] * TILE + positions[..., 0]).reshape(-1).astype(jnp.int32)
    scan_columns = (jnp.arange(N_TX, dtype=jnp.int32)[None, :, None] * TILE + positions[..., 1]).reshape(-1).astype(jnp.int32)
    measured_flat_rows = measured.reshape(-1, PATCH_WIDTH, PATCH_WIDTH)
    count = N_TY * N_TX * P_DEV
    zero = jnp.zeros((), jnp.int32)
    for step in range(ITERS):
        padded_object = jnp.pad(object_planes, ((0, 0), (0, 0), (0, PATCH_WIDTH), (0, PATCH_WIDTH)))

        def visit_position(carry, scan_entry):
            object_gradient, probe_gradient = carry
            scan_row, scan_column, measured_intensity = scan_entry
            start = (zero, zero, scan_row, scan_column)
            object_patch = lax.dynamic_slice(padded_object, start, (SLICES, 2, PATCH_WIDTH, PATCH_WIDTH))
            loss_value_total, backward_field = jax.vjp(lambda patch_argument, probe_argument: single_patch_loss(patch_argument, probe_argument, measured_intensity), object_patch, probe)
            g_patch, g_probe = backward_field(jnp.ones_like(loss_value_total))
            old = lax.dynamic_slice(object_gradient, start, (SLICES, 2, PATCH_WIDTH, PATCH_WIDTH))
            object_gradient = lax.dynamic_update_slice(object_gradient, old + g_patch, start)
            return ((object_gradient, probe_gradient + g_probe), None)
        (object_gradient, probe_gradient), unused_slot = lax.scan(visit_position, (jnp.zeros_like(padded_object), jnp.zeros_like(probe)), (scan_rows, scan_columns, measured_flat_rows))
        object_gradient = object_gradient[:, :, :OBJ_R, :OBJ_C]
        object_planes = object_planes - 0.1 * object_gradient
        probe = probe - 0.5 / count * probe_gradient
    return (object_planes, probe)
```

```python
import math

import jax
import jax.numpy as jnp
import numpy as np
from jax import lax
from jax.experimental import pallas as pl
from jax.experimental.pallas import tpu as pltpu
from jax.sharding import PartitionSpec as P
import ml_dtypes

MESH = pl.DeviceIdType.MESH
F32 = jnp.float32
BF16 = jnp.bfloat16
N = 256
H = 128
ITERS = 2
RB = 16
CHUNKS = [(s, p, h * H, H) for s in (1, 0) for p in (0, 1) for h in (0, 1)]
NCH = len(CHUNKS)
OBJ_STEP = 0.1


def real_form(block):
    top = np.concatenate([block.real, -block.imag], axis=1)
    low = np.concatenate([block.imag, block.real], axis=1)
    return np.concatenate([top, low], axis=0)


def tables():
    k = np.arange(N)
    dft = np.exp(-2j * math.pi * ((k[:, None] * k[None, :]) % N) / N) / math.sqrt(N)
    chirp = np.exp(1j * math.pi * ((k * k) % (2 * N)) / N)
    prop = np.exp(-0.25j * math.pi) * chirp[:, None] * dft * chirp[None, :]
    kinds = []
    for kind in range(4):
        pars = []
        for par in (0, 1):
            if kind < 2:
                mat = real_form(prop[par::2, :H])
            else:
                mat = real_form(dft[:H, par::2])
            if kind % 2:
                mat = mat.T
            mat = mat.astype(np.float32)
            hi = mat.astype(ml_dtypes.bfloat16)
            lo = (mat - hi.astype(np.float32)).astype(ml_dtypes.bfloat16)
            pars.append(np.stack([hi, lo]))
        kinds.append(np.stack(pars))
    return np.stack(kinds)


def shuffles():
    perm = np.zeros((N, N), np.float32)
    j = np.arange(H)
    perm[j, 2 * j] = 1
    perm[H + j, 2 * j + 1] = 1
    return np.stack([perm, perm.T]).astype(ml_dtypes.bfloat16)


def split(x):
    hi = x.astype(BF16)
    return hi, (x - hi.astype(F32)).astype(BF16)


def split3(x):
    hi = x.astype(BF16)
    rest = x - hi.astype(F32)
    mid = rest.astype(BF16)
    return hi, mid, (rest - mid.astype(F32)).astype(BF16)


def dot(a, b):
    return jnp.dot(a, b, preferred_element_type=F32)


def permute_rows(perm, x):
    hi, mid, lo = split3(x)
    return dot(perm, hi) + dot(perm, mid) + dot(perm, lo)


def permute_cols(perm, x):
    hi, mid, lo = split3(x)
    return dot(hi, perm) + dot(mid, perm) + dot(lo, perm)


def blocks(count, body):
    def step(b, carry):
        body(pl.multiple_of(b * RB, RB))
        return carry

    lax.fori_loop(0, count, step, 0)


def make_kernel(n_ty, n_tx):
    ny = 4 if n_tx == 16 else 2
    nx = n_tx // ny
    nz = n_ty // 2
    xr = N // nx
    yr = xr // ny

    def kernel(pos, obj, probe_in, meas_in, mats_in, perm_in, obj_out, probe_out,
               tor, tbc1, tbc2, gor, gbc, ra, rb, rc, t0, t1, pw, gp, gsum, probe,
               dhi, dlo, lhi, llo, gbuf, rbuf, psi, meas, mats, perm, stage, result,
               r0, r1, r2, rz, send, recv, local):
        ty = lax.axis_index("ty")
        tx = lax.axis_index("tx")
        up = (lax.rem(ty + n_ty - 1, n_ty), tx)
        down = (lax.rem(ty + 1, n_ty), tx)
        left = (ty, lax.rem(tx + n_tx - 1, n_tx))
        right = (ty, lax.rem(tx + 1, n_tx))
        core = lax.rem(ty, 2)
        z = lax.div(ty, 2)
        x = lax.div(tx, ny)
        y = lax.rem(tx, ny)
        mate = (ty + 1 - 2 * core, tx)
        xs = [(ty, lax.rem(x + d, nx) * ny + y) for d in range(1, nx)]
        ys = [(ty, x * ny + lax.rem(y + d, ny)) for d in range(1, ny)]
        zs = [(lax.rem(z + d, nz) * 2 + core, tx) for d in range(1, nz)]
        has_above = jnp.where(ty > 0, 1.0, 0.0).astype(F32)
        has_below = jnp.where(ty < n_ty - 1, 1.0, 0.0).astype(F32)
        has_left = jnp.where(tx > 0, 1.0, 0.0).astype(F32)
        has_right = jnp.where(tx < n_tx - 1, 1.0, 0.0).astype(F32)

        used = [0]

        def remote(src, dst, device):
            index = used[0]
            used[0] += 1
            return pltpu.make_async_remote_copy(
                src_ref=src, dst_ref=dst, send_sem=send.at[index], recv_sem=recv.at[index],
                device_id=device, device_id_type=MESH)

        def rows_of(chunk):
            s, p, r, n = chunk
            return s, p, pl.ds(r, n)

        loads = [
            pltpu.make_async_copy(obj.at[1], stage, local.at[0]),
            pltpu.make_async_copy(perm_in, perm, local.at[1]),
            pltpu.make_async_copy(obj.at[0], tor.at[0, 0], local.at[2]),
            pltpu.make_async_copy(probe_in, probe.at[0], local.at[3]),
            pltpu.make_async_copy(mats_in, mats, local.at[4]),
            pltpu.make_async_copy(meas_in, meas, local.at[5]),
        ]
        for copy in loads:
            copy.start()

        barrier = pltpu.get_barrier_semaphore()
        partners = [left, right, up, down] + xs + ys + zs
        for device in partners:
            pl.semaphore_signal(barrier, inc=1, device_id=device, device_id_type=MESH)
        pl.semaphore_wait(barrier, len(partners))

        first_chunks = CHUNKS[NCH // 2:] + CHUNKS[:NCH // 2]
        own_left, own_up, right_up = [], [], []
        for chunk in first_chunks:
            s, p, rows = rows_of(chunk)
            src = obj.at[0, p, rows] if s == 0 else tor.at[0, 1, p, rows]
            own_left.append(remote(src, tor.at[1, s, p, rows], left))
            own_up.append(remote(src, tbc1.at[0, s, p, rows], up))
            right_up.append(remote(tor.at[1, s, p, rows], tbc1.at[1, s, p, rows], up))
        for i in range(NCH // 2):
            own_left[i].start()
            own_up[i].start()
        loads[0].wait()
        loads[1].wait()
        for p in (0, 1):
            tor[0, 1, p] = permute_cols(perm[1], permute_rows(perm[0], stage[p]))
            for i in range(NCH // 2 + p * NCH // 4, NCH // 2 + (p + 1) * NCH // 4):
                own_left[i].start()
                own_up[i].start()

        row_in_block = lax.broadcasted_iota(jnp.int32, (RB, N), 0)
        col_index = lax.broadcasted_iota(jnp.int32, (RB, N), 1)
        col_half = lax.broadcasted_iota(jnp.int32, (RB, H), 1)
        row_half = lax.broadcasted_iota(jnp.int32, (RB, H), 0)
        row_sign = jnp.where(lax.rem(row_in_block, 2) == 1, -1.0, 1.0).astype(F32)
        col_sign = jnp.where(lax.rem(col_half, 2) == 1, -1.0, 1.0).astype(F32)
        offsets = [(pos[0], pos[1]), (pos[2], pos[3])]

        def window(tbc, s, p, rows, cols, row_ok, col_ok):
            upper = jnp.where(col_ok, tor[0, s, p, rows, cols], has_right * tor[1, s, p, rows, cols])
            lower = jnp.where(col_ok, tbc[0, s, p, rows, cols], has_right * tbc[1, s, p, rows, cols])
            return jnp.where(row_ok, upper, has_below * lower)

        def put_d(par, rr, k, cols, value):
            hi, lo = split(value)
            rows = pl.ds(rr + k * H, RB)
            dhi[par, rows, cols] = hi
            dlo[par, rows, cols] = lo

        def put_l(cp, rows, k, value):
            hi, lo = split(value)
            cols = pl.ds(k * H, H)
            lhi[cp, rows, cols] = hi
            llo[cp, rows, cols] = lo

        def left_product(kind):
            for par in (0, 1):
                a_hi, a_lo = mats[kind, par, 0], mats[kind, par, 1]
                gbuf[par] = dot(a_lo, dhi[par]) + dot(a_hi, dlo[par]) + dot(a_hi, dhi[par])

        def right_product(kind, out):
            for cp in (0, 1):
                b_hi, b_lo = mats[kind, cp, 0], mats[kind, cp, 1]
                out[cp] = dot(lhi[cp], b_lo) + dot(llo[cp], b_hi) + dot(lhi[cp], b_hi)

        def col_split(signed):
            def body(rr):
                for par in (0, 1):
                    for q in (0, 1):
                        for k in (0, 1):
                            low = gbuf[par, pl.ds(rr + k * H, RB), pl.ds(q * N, H)]
                            high = gbuf[par, pl.ds(rr + k * H, RB), pl.ds(q * N + H, H)]
                            if signed:
                                high = high * col_sign
                            rows = pl.ds(rr + q * N + par * H, RB)
                            put_l(0, rows, k, low + high)
                            put_l(1, rows, k, low - high)
            blocks(H // RB, body)

        def col_join(signed):
            def body(rr):
                for par in (0, 1):
                    for q in (0, 1):
                        rows = pl.ds(rr + q * N + par * H, RB)
                        for k in (0, 1):
                            even = rbuf[0, rows, pl.ds(k * H, H)]
                            odd = rbuf[1, rows, pl.ds(k * H, H)]
                            high = even - odd
                            if signed:
                                high = high * col_sign
                            put_d(par, rr, k, pl.ds(q * N, H), even + odd)
                            put_d(par, rr, k, pl.ds(q * N + H, H), high)
            blocks(H // RB, body)

        def roll_probe(step):
            for q in (0, 1):
                for k in (0, 1):
                    moved = pltpu.roll(probe[step, k], offsets[q][0], 0)
                    pw[q, k] = pltpu.roll(moved, offsets[q][1], 1)

        def forward_first(tbc):
            def body(rr):
                for q in (0, 1):
                    r, c = offsets[q]
                    col_ok = col_index >= c
                    fields = []
                    for half in (0, 1):
                        rows = pl.ds(rr + half * H, RB)
                        row_ok = row_in_block + (rr + half * H) >= r
                        tr = window(tbc, 0, 0, rows, slice(None), row_ok, col_ok)
                        ti = window(tbc, 0, 1, rows, slice(None), row_ok, col_ok)
                        t0[q, 0, rows] = tr
                        t0[q, 1, rows] = ti
                        pr, pi = pw[q, 0, rows], pw[q, 1, rows]
                        fields.append((pr * tr - pi * ti, pr * ti + pi * tr))
                    for k in (0, 1):
                        high = fields[1][k] * row_sign
                        put_d(0, rr, k, pl.ds(q * N, N), fields[0][k] + high)
                        put_d(1, rr, k, pl.ds(q * N, N), fields[0][k] - high)
            blocks(H // RB, body)
            left_product(0)
            col_split(True)
            right_product(1, psi)

        def forward_rest(tbc):
            def body(rr):
                for q in (0, 1):
                    r, c = offsets[q]
                    for par in (0, 1):
                        trows = pl.ds(rr + par * H, RB)
                        rows = pl.ds(rr + q * N + par * H, RB)
                        row_ok = 2 * (row_half + rr) + par >= r
                        for cp in (0, 1):
                            col_ok = 2 * col_half + cp >= c
                            cols = pl.ds(cp * H, H)
                            tr = window(tbc, 1, 0, trows, cols, row_ok, col_ok)
                            ti = window(tbc, 1, 1, trows, cols, row_ok, col_ok)
                            t1[q, 0, trows, cols] = tr
                            t1[q, 1, trows, cols] = ti
                            fr = psi[cp, rows, pl.ds(0, H)]
                            fi = psi[cp, rows, pl.ds(H, H)]
                            put_l(cp, rows, 0, fr * tr - fi * ti)
                            put_l(cp, rows, 1, fr * ti + fi * tr)
            blocks(H // RB, body)
            right_product(3, rbuf)
            col_join(False)
            left_product(2)

        def backward_first():
            def body(rr):
                for q in (0, 1):
                    cols = pl.ds(q * N, N)
                    er, ei = gbuf[0, pl.ds(rr, RB), cols], gbuf[0, pl.ds(rr + H, RB), cols]
                    odr, odi = gbuf[1, pl.ds(rr, RB), cols], gbuf[1, pl.ds(rr + H, RB), cols]
                    halves = []
                    for half, (fr, fi) in enumerate(((er + odr, ei + odi), (er - odr, ei - odi))):
                        m = meas[q, pl.ds(rr + half * H, RB)]
                        weight = 1.0 - m * lax.rsqrt(fr * fr + fi * fi + 1.0)
                        halves.append((weight * fr, weight * fi))
                    for k in (0, 1):
                        put_d(0, rr, k, cols, halves[0][k] + halves[1][k])
                        put_d(1, rr, k, cols, halves[0][k] - halves[1][k])
            blocks(H // RB, body)
            left_product(3)
            col_split(False)
            right_product(2, rbuf)

        def scatter(s, p, rows, cols, values, row_oks, col_oks):
            zero = jnp.zeros_like(values[0])
            upper = [jnp.where(row_oks[q], values[q], zero) for q in (0, 1)]
            lower = [values[q] - upper[q] for q in (0, 1)]
            for part, dst in ((upper, gor), (lower, gbc)):
                kept = [jnp.where(col_oks[q], part[q], zero) for q in (0, 1)]
                dst[0, s, p, rows, cols] = kept[0] + kept[1]
                dst[1, s, p, rows, cols] = (part[0] - kept[0]) + (part[1] - kept[1])

        def backward_second():
            def body(rr):
                for par in (0, 1):
                    trows = pl.ds(rr + par * H, RB)
                    row_oks = [2 * (row_half + rr) + par >= offsets[q][0] for q in (0, 1)]
                    for cp in (0, 1):
                        col_oks = [2 * col_half + cp >= offsets[q][1] for q in (0, 1)]
                        cols = pl.ds(cp * H, H)
                        grads = []
                        for q in (0, 1):
                            rows = pl.ds(rr + q * N + par * H, RB)
                            gr, gi = rbuf[cp, rows, pl.ds(0, H)], rbuf[cp, rows, pl.ds(H, H)]
                            fr, fi = psi[cp, rows, pl.ds(0, H)], psi[cp, rows, pl.ds(H, H)]
                            tr, ti = t1[q, 0, trows, cols], t1[q, 1, trows, cols]
                            grads.append((gr * fr + gi * fi, gi * fr - gr * fi))
                            put_l(cp, rows, 0, gr * tr + gi * ti)
                            put_l(cp, rows, 1, gi * tr - gr * ti)
                        for k in (0, 1):
                            scatter(1, k, trows, cols, [g[k] for g in grads], row_oks, col_oks)
            blocks(H // RB, body)

        def backward_last():
            right_product(0, rbuf)
            col_join(True)
            left_product(1)

            def body(rr):
                col_oks = [col_index >= offsets[q][1] for q in (0, 1)]
                for half in (0, 1):
                    rows = pl.ds(rr + half * H, RB)
                    row_oks = [row_in_block + (rr + half * H) >= offsets[q][0] for q in (0, 1)]
                    grads = []
                    for q in (0, 1):
                        cols = pl.ds(q * N, N)
                        er, ei = gbuf[0, pl.ds(rr, RB), cols], gbuf[0, pl.ds(rr + H, RB), cols]
                        odr, odi = gbuf[1, pl.ds(rr, RB), cols], gbuf[1, pl.ds(rr + H, RB), cols]
                        if half:
                            ur, ui = (er - odr) * row_sign, (ei - odi) * row_sign
                        else:
                            ur, ui = er + odr, ei + odi
                        pr, pi = pw[q, 0, rows], pw[q, 1, rows]
                        tr, ti = t0[q, 0, rows], t0[q, 1, rows]
                        grads.append((ur * pr + ui * pi, ui * pr - ur * pi))
                        gp[q, 0, rows] = ur * tr + ui * ti
                        gp[q, 1, rows] = ui * tr - ur * ti
                    for k in (0, 1):
                        scatter(0, k, rows, slice(None), [g[k] for g in grads], row_oks, col_oks)
            blocks(H // RB, body)

        def sum_probe():
            for k in (0, 1):
                parts = []
                for q in (0, 1):
                    back = pltpu.roll(gp[q, k], lax.rem(N - offsets[q][0], N), 0)
                    parts.append(pltpu.roll(back, lax.rem(N - offsets[q][1], N), 1))
                gsum[k] = parts[0] + parts[1]

        def reduction(step):
            buf = step
            c0 = remote(gsum.at[1 - core], r0.at[buf], mate)
            c1 = [remote(r0.at[buf, pl.ds(pl.multiple_of(lax.rem(x + d, nx) * xr, xr), xr)],
                         r1.at[buf, d - 1], xs[d - 1]) for d in range(1, nx)]
            c2 = [remote(r1.at[buf, nx - 1, pl.ds(pl.multiple_of(lax.rem(y + d, ny) * yr, yr), yr)],
                         r2.at[buf, d - 1], ys[d - 1]) for d in range(1, ny)]
            c3 = [remote(rz.at[buf, z], rz.at[buf, z], zs[d - 1]) for d in range(1, nz)]
            base_x = pl.multiple_of(x * xr, xr)
            base_y = pl.multiple_of(y * yr, yr)
            base = pl.multiple_of(x * xr + y * yr, yr)
            mine = probe.at[step + 1, core, pl.ds(base, yr)]
            strip = probe.at[step + 1, core, pl.ds(base_x, xr)]
            plane = probe.at[step + 1, core]
            c4 = [remote(mine, mine, ys[d - 1]) for d in range(1, ny)]
            c5 = [remote(strip, strip, xs[d - 1]) for d in range(1, nx)]
            c6 = remote(plane, plane, mate)

            def a0():
                c0.start()

            def a1():
                c0.wait_recv()
                r0[buf] = r0[buf] + gsum[core]
                for c in c1:
                    c.start()

            def a2():
                total = r0[buf, pl.ds(base_x, xr)]
                for i, c in enumerate(c1):
                    c.wait_recv()
                    total = total + r1[buf, i]
                r1[buf, nx - 1] = total
                for c in c2:
                    c.start()

            def a3():
                total = r1[buf, nx - 1, pl.ds(base_y, yr)]
                for i, c in enumerate(c2):
                    c.wait_recv()
                    total = total + r2[buf, i]
                rz[buf, z] = total
                for c in c3:
                    c.start()

            def a4():
                for c in c3:
                    c.wait_recv()
                total = rz[buf, 0]
                for i in range(1, nz):
                    total = total + rz[buf, i]
                scale = 0.5 / (n_ty * n_tx * 2)
                probe[step + 1, core, pl.ds(base, yr)] = probe[step, core, pl.ds(base, yr)] - scale * total
                for c in c4:
                    c.start()

            def a5():
                for c in c4:
                    c.wait_recv()
                for c in c5:
                    c.start()

            def a6():
                for c in c5:
                    c.wait_recv()
                c6.start()

            def a7():
                c6.wait_recv()
                for c in [c0, c6] + c1 + c2 + c3 + c4 + c5:
                    c.wait_send()

            return [a0, a1, a2, a3, a4, a5, a6, a7]

        def grads_down(step):
            return [remote(gbc.at[:, s, p, rows], ra.at[step, :, s, p, rows], down)
                    for s, p, rows in map(rows_of, CHUNKS)]

        half = NCH // 2
        for i in range(half):
            own_left[i].wait_recv()
            right_up[i].start()
        loads[2].wait()
        loads[3].wait()
        roll_probe(0)
        own_left[half].wait_recv()
        right_up[half].start()
        for i in range(half):
            own_up[i].wait_recv()
            right_up[i].wait_recv()
        loads[4].wait()
        forward_first(tbc1)
        for i in range(half + 1, NCH):
            own_left[i].wait_recv()
            right_up[i].start()
        for i in range(half, NCH):
            own_up[i].wait_recv()
            right_up[i].wait_recv()
        loads[5].wait()
        forward_rest(tbc1)
        backward_first()
        backward_second()
        for c in own_left + own_up + right_up:
            c.wait_send()

        a_sends = grads_down(0)
        b_right, b_left, c_up = [], [], []
        for s, p, rows in map(rows_of, CHUNKS):
            b_right.append(remote(gor.at[1, s, p, rows], rb.at[0, s, p, rows], right))
            b_left.append(remote(gor.at[0, s, p, rows], rc.at[s, p, rows], left))
            c_up.append(remote(tor.at[:, s, p, rows], tbc2.at[:, s, p, rows], up))
        for i in range(half):
            a_sends[i].start()
        backward_last()
        for i in range(half, NCH):
            a_sends[i].start()
        sum_probe()
        actions = reduction(0)
        actions.pop(0)()

        def add_above(i, step):
            s, p, rows = rows_of(CHUNKS[i])
            a_sends[i].wait_recv()
            for part in (0, 1):
                gor[part, s, p, rows] = gor[part, s, p, rows] + has_above * ra[step, part, s, p, rows]

        def mid_b(i):
            add_above(i, 0)
            b_right[i].start()
            b_left[i].start()

        def mid_c(i):
            s, p, rows = rows_of(CHUNKS[i])
            b_right[i].wait_recv()
            b_left[i].wait_recv()
            tor[0, s, p, rows] = tor[0, s, p, rows] - OBJ_STEP * (
                gor[0, s, p, rows] + has_left * rb[0, s, p, rows])
            tor[1, s, p, rows] = tor[1, s, p, rows] - OBJ_STEP * (
                gor[1, s, p, rows] + has_right * rc[s, p, rows])
            c_up[i].start()

        mid_b(0)
        for i in range(1, NCH):
            mid_b(i)
            mid_c(i - 1)
            if actions:
                actions.pop(0)()
        mid_c(NCH - 1)
        while actions:
            actions.pop(0)()
        roll_probe(1)
        for c in c_up:
            c.wait_recv()
        for c in a_sends + b_right + b_left:
            c.wait_send()

        forward_first(tbc2)
        forward_rest(tbc2)
        backward_first()
        backward_second()
        for c in c_up:
            c.wait_send()
        a_sends = grads_down(1)
        b_right = [remote(gor.at[1, s, p, rows], rb.at[1, s, p, rows], right)
                   for s, p, rows in map(rows_of, CHUNKS)]
        for i in range(half):
            a_sends[i].start()
        backward_last()
        for i in range(half, NCH):
            a_sends[i].start()
        sum_probe()
        actions = reduction(1)
        actions.pop(0)()

        def end_b(i):
            add_above(i, 1)
            b_right[i].start()

        def end_c(i):
            s, p, rows = rows_of(CHUNKS[i])
            b_right[i].wait_recv()
            value = tor[0, s, p, rows] - OBJ_STEP * (gor[0, s, p, rows] + has_left * rb[1, s, p, rows])
            if s == 0:
                result[0, p, rows] = value
            else:
                stage[p, rows] = value

        stores = []
        end_b(0)
        for i in range(1, NCH):
            end_b(i)
            end_c(i - 1)
            if actions:
                actions.pop(0)()
            if i == half + 1:
                for p in (0, 1):
                    result[1, p] = permute_cols(perm[0], permute_rows(perm[1], stage[p]))
                stores.append(pltpu.make_async_copy(result.at[1], obj_out.at[1], local.at[6]))
                stores[-1].start()
        end_c(NCH - 1)
        stores.append(pltpu.make_async_copy(result.at[0], obj_out.at[0], local.at[7]))
        stores[-1].start()
        while actions:
            actions.pop(0)()
        stores.append(pltpu.make_async_copy(probe.at[2], probe_out, local.at[8]))
        stores[-1].start()
        for c in a_sends + b_right:
            c.wait_send()
        for copy in stores:
            copy.wait()

    copies = 3 * NCH + 4 * NCH + 2 * NCH + 2 * (2 + 2 * (nx - 1) + 2 * (ny - 1) + nz - 1)
    field = (2, 2, N, N)
    scratch = dict(
        tor=pltpu.VMEM((2,) + field, F32),
        tbc1=pltpu.VMEM((2,) + field, F32),
        tbc2=pltpu.VMEM((2,) + field, F32),
        gor=pltpu.VMEM((2,) + field, F32),
        gbc=pltpu.VMEM((2,) + field, F32),
        ra=pltpu.VMEM((2, 2) + field, F32),
        rb=pltpu.VMEM((2,) + field, F32),
        rc=pltpu.VMEM(field, F32),
        t0=pltpu.VMEM(field, F32),
        t1=pltpu.VMEM(field, F32),
        pw=pltpu.VMEM(field, F32),
        gp=pltpu.VMEM(field, F32),
        gsum=pltpu.VMEM((2, N, N), F32),
        probe=pltpu.VMEM((3, 2, N, N), F32),
        dhi=pltpu.VMEM((2, N, 2 * N), BF16),
        dlo=pltpu.VMEM((2, N, 2 * N), BF16),
        lhi=pltpu.VMEM((2, 2 * N, N), BF16),
        llo=pltpu.VMEM((2, 2 * N, N), BF16),
        gbuf=pltpu.VMEM((2, N, 2 * N), F32),
        rbuf=pltpu.VMEM((2, 2 * N, N), F32),
        psi=pltpu.VMEM((2, 2 * N, N), F32),
        meas=pltpu.VMEM((2, N, N), F32),
        mats=pltpu.VMEM((4, 2, 2, N, N), BF16),
        perm=pltpu.VMEM((2, N, N), BF16),
        stage=pltpu.VMEM((2, N, N), F32),
        result=pltpu.VMEM(field, F32),
        r0=pltpu.VMEM((2, N, N), F32),
        r1=pltpu.VMEM((2, nx, xr, N), F32),
        r2=pltpu.VMEM((2, ny - 1, yr, N), F32),
        rz=pltpu.VMEM((2, nz, yr, N), F32),
        send=pltpu.SemaphoreType.DMA((copies,)),
        recv=pltpu.SemaphoreType.DMA((copies,)),
        local=pltpu.SemaphoreType.DMA((9,)),
    )
    return kernel, list(scratch.values())


def solution(mesh):
    n_ty, n_tx = mesh.shape["ty"], mesh.shape["tx"]
    kernel, scratch = make_kernel(n_ty, n_tx)
    mats, perm = tables(), shuffles()

    def body(object_planes, probe, positions, measured):
        return pl.pallas_call(
            kernel,
            out_shape=(
                jax.ShapeDtypeStruct(object_planes.shape, F32),
                jax.ShapeDtypeStruct(probe.shape, F32),
            ),
            in_specs=[pl.BlockSpec(memory_space=pltpu.SMEM)] + [pl.BlockSpec(memory_space=pl.ANY)] * 5,
            out_specs=(pl.BlockSpec(memory_space=pl.ANY), pl.BlockSpec(memory_space=pl.ANY)),
            scratch_shapes=scratch,
            compiler_params=pltpu.CompilerParams(
                collective_id=0, has_side_effects=True, vmem_limit_bytes=56 * 1024 * 1024),
        )(positions.reshape(4), object_planes, probe, measured[0, 0], jnp.asarray(mats), jnp.asarray(perm))

    return jax.shard_map(
        body,
        mesh=mesh,
        in_specs=(
            P(None, None, "ty", "tx"),
            P(),
            P("ty", "tx", None, None),
            P("ty", "tx", None, None, None),
        ),
        out_specs=(P(None, None, "ty", "tx"), P()),
        check_vma=False,
    )
```

```python
import math

import jax
import jax.numpy as jnp
import numpy as np
from jax import lax
from jax.experimental import pallas as pl
from jax.experimental.pallas import tpu as pltpu
from jax.sharding import PartitionSpec as P
import ml_dtypes

MESH = pl.DeviceIdType.MESH
F32 = jnp.float32
BF16 = jnp.bfloat16
N = 256
H = 128
ITERS = 2
RB = 16
CR = 64
QUARTERS = N // CR
GATHER = [(0, 0), (0, 1), (1, 0), (1, 1)]
MID = [(1, 0), (0, 0), (0, 1), (1, 1)]
LAST = [(1, 0), (1, 1), (0, 0), (0, 1)]
NCH = 4 * QUARTERS
SENDERS = 24
ARRIVALS = 112
MID_PLAN = ("r", "A2", "r", "A4", "B2", "r", "r", "A3", "B4", "C3", "r", "A3", "B4", "C3", "r", "B4", "C4", "r", "B2", "C3", "r", "C1")
END_PLAN = ("r", "B3", "r", "B3", "r", "B2", "K8", "r", "B2", "r", "L8", "B2", "r", "B2", "r", "B2", "L8", "r", "E4", "r", "E4", "r", "E8")
OBJ_STEP = 0.1


def real_form(block):
    top = np.concatenate([block.real, -block.imag], axis=1)
    low = np.concatenate([block.imag, block.real], axis=1)
    return np.concatenate([top, low], axis=0)


def tables():
    k = np.arange(N)
    dft = np.exp(-2j * math.pi * ((k[:, None] * k[None, :]) % N) / N) / math.sqrt(N)
    chirp = np.exp(1j * math.pi * ((k * k) % (2 * N)) / N)
    prop = np.exp(-0.25j * math.pi) * chirp[:, None] * dft * chirp[None, :]
    kinds = []
    for kind in range(4):
        pars = []
        for par in (0, 1):
            if kind < 2:
                mat = real_form(prop[par::2, :H])
            else:
                mat = real_form(dft[:H, par::2])
            if kind % 2:
                mat = mat.T
            mat = mat.astype(np.float32)
            hi = mat.astype(ml_dtypes.bfloat16)
            lo = (mat - hi.astype(np.float32)).astype(ml_dtypes.bfloat16)
            pars.append(np.stack([hi, lo]))
        kinds.append(np.stack(pars))
    return np.stack(kinds)


def shuffles():
    perm = np.zeros((N, N), np.float32)
    j = np.arange(H)
    perm[j, 2 * j] = 1
    perm[H + j, 2 * j + 1] = 1
    return np.stack([perm, perm.T]).astype(ml_dtypes.bfloat16)


def split(x):
    hi = x.astype(BF16)
    return hi, (x - hi.astype(F32)).astype(BF16)


def split3(x):
    hi = x.astype(BF16)
    rest = x - hi.astype(F32)
    mid = rest.astype(BF16)
    return hi, mid, (rest - mid.astype(F32)).astype(BF16)


def dot(a, b):
    return jnp.dot(a, b, preferred_element_type=F32)


def permute_rows(perm, x):
    hi, mid, lo = split3(x)
    return dot(perm, hi) + dot(perm, mid) + dot(perm, lo)


def permute_cols(perm, x):
    hi, mid, lo = split3(x)
    return dot(hi, perm) + dot(mid, perm) + dot(lo, perm)


def blocks(count, body):
    def step(b, carry):
        body(pl.multiple_of(b * RB, RB))
        return carry

    lax.fori_loop(0, count, step, 0, unroll=True)


def make_kernel(n_ty, n_tx):
    ny = 4 if n_tx == 16 else 2
    nx = n_tx // ny
    nz = n_ty // 2
    xr = N // nx
    zr = xr // nz

    def kernel(pos, obj, probe_in, meas_in, mats_in, perm_in, obj_out, probe_out,
               tor, tbc1, tbc2, gor, gbc, ra, rb, rc, t0, t1, pw, gp, gsum, probe,
               dhi, dlo, lhi, llo, gbuf, rbuf, psi, meas, mats, perm, stage, result,
               r0, r1, r2, ry, send, recv, local):
        ty = lax.axis_index("ty")
        tx = lax.axis_index("tx")
        up = (lax.rem(ty + n_ty - 1, n_ty), tx)
        down = (lax.rem(ty + 1, n_ty), tx)
        left = (ty, lax.rem(tx + n_tx - 1, n_tx))
        right = (ty, lax.rem(tx + 1, n_tx))
        core = lax.rem(ty, 2)
        z = lax.div(ty, 2)
        x = lax.div(tx, ny)
        y = lax.rem(tx, ny)
        mate = (ty + 1 - 2 * core, tx)
        xs = [(ty, lax.rem(x + d, nx) * ny + y) for d in range(1, nx)]
        ys = [(ty, x * ny + lax.rem(y + d, ny)) for d in range(1, ny)]
        zs = [(lax.rem(z + d, nz) * 2 + core, tx) for d in range(1, nz)]
        has_above = jnp.where(ty > 0, 1.0, 0.0).astype(F32)
        has_below = jnp.where(ty < n_ty - 1, 1.0, 0.0).astype(F32)
        has_left = jnp.where(tx > 0, 1.0, 0.0).astype(F32)
        has_right = jnp.where(tx < n_tx - 1, 1.0, 0.0).astype(F32)

        senders, arrivals = iter(range(SENDERS)), iter(range(ARRIVALS))

        def remote(src, dst, device, out, into):
            return pltpu.make_async_remote_copy(
                src_ref=src, dst_ref=dst, send_sem=send.at[out], recv_sem=recv.at[into],
                device_id=device, device_id_type=MESH)

        def landed(ref, into):
            pltpu.make_async_copy(ref, ref, recv.at[into]).wait()

        def gone(ref, out):
            pltpu.make_async_copy(ref, ref, send.at[out]).wait()

        def take(source, count):
            return [next(source) for _ in range(count)]

        def chunks(order):
            return [(s, p, pl.ds(r * CR, CR)) for s, p in order for r in range(QUARTERS)]

        loads = [
            pltpu.make_async_copy(obj.at[1], stage, local.at[0]),
            pltpu.make_async_copy(perm_in, perm, local.at[1]),
            pltpu.make_async_copy(obj.at[0], tor.at[0, 0], local.at[2]),
            pltpu.make_async_copy(probe_in, probe.at[0], local.at[3]),
            pltpu.make_async_copy(mats_in, mats, local.at[4]),
            pltpu.make_async_copy(meas_in.at[0, 0], meas, local.at[5]),
        ]
        for copy in loads:
            copy.start()

        barrier = pltpu.get_barrier_semaphore()
        partners = [left, right, up, down] + xs + ys + zs
        for device in partners:
            pl.semaphore_signal(barrier, inc=1, device_id=device, device_id_type=MESH)
        pl.semaphore_wait(barrier, len(partners))

        own_left, own_up, right_up = [], [], []
        out_left, out_up, out_right = take(senders, 3)
        in_right, in_below, in_corner = take(arrivals, NCH), take(arrivals, 2), take(arrivals, 2)
        for i, (s, p, rows) in enumerate(chunks(GATHER)):
            src = obj.at[0, p, rows] if s == 0 else tor.at[0, 1, p, rows]
            own_left.append(remote(src, tor.at[1, s, p, rows], left, out_left, in_right[i]))
            own_up.append(remote(src, tbc1.at[0, s, p, rows], up, out_up, in_below[s]))
            right_up.append(remote(tor.at[1, s, p, rows], tbc1.at[1, s, p, rows], up, out_right, in_corner[s]))
        for i in range(NCH // 2):
            own_left[i].start()
            own_up[i].start()
        loads[0].wait()
        loads[1].wait()
        for p in (0, 1):
            tor[0, 1, p] = permute_cols(perm[1], permute_rows(perm[0], stage[p]))
            for i in range((2 + p) * QUARTERS, (3 + p) * QUARTERS):
                own_left[i].start()
                own_up[i].start()

        row_in_block = lax.broadcasted_iota(jnp.int32, (RB, N), 0)
        col_index = lax.broadcasted_iota(jnp.int32, (RB, N), 1)
        col_half = lax.broadcasted_iota(jnp.int32, (RB, H), 1)
        row_half = lax.broadcasted_iota(jnp.int32, (RB, H), 0)
        row_sign = jnp.where(lax.rem(row_in_block, 2) == 1, -1.0, 1.0).astype(F32)
        col_sign = jnp.where(lax.rem(col_half, 2) == 1, -1.0, 1.0).astype(F32)
        offsets = [(pos[0, 0, 0, 0], pos[0, 0, 0, 1]), (pos[0, 0, 1, 0], pos[0, 0, 1, 1])]

        def window(tbc, s, p, rows, cols, row_ok, col_ok):
            upper = jnp.where(col_ok, tor[0, s, p, rows, cols], has_right * tor[1, s, p, rows, cols])
            lower = jnp.where(col_ok, tbc[0, s, p, rows, cols], has_right * tbc[1, s, p, rows, cols])
            return jnp.where(row_ok, upper, has_below * lower)

        def put_d(par, rr, k, cols, value):
            hi, lo = split(value)
            rows = pl.ds(rr + k * H, RB)
            dhi[par, rows, cols] = hi
            dlo[par, rows, cols] = lo

        def put_l(cp, rows, k, value):
            hi, lo = split(value)
            cols = pl.ds(k * H, H)
            lhi[cp, rows, cols] = hi
            llo[cp, rows, cols] = lo

        def left_product(kind):
            for par in (0, 1):
                a_hi, a_lo = mats[kind, par, 0], mats[kind, par, 1]
                gbuf[par] = dot(a_lo, dhi[par]) + dot(a_hi, dlo[par]) + dot(a_hi, dhi[par])

        def right_product(kind, out):
            for cp in (0, 1):
                b_hi, b_lo = mats[kind, cp, 0], mats[kind, cp, 1]
                out[cp] = dot(lhi[cp], b_lo) + dot(llo[cp], b_hi) + dot(lhi[cp], b_hi)

        def col_split(signed):
            def body(rr):
                for par in (0, 1):
                    for q in (0, 1):
                        for k in (0, 1):
                            low = gbuf[par, pl.ds(rr + k * H, RB), pl.ds(q * N, H)]
                            high = gbuf[par, pl.ds(rr + k * H, RB), pl.ds(q * N + H, H)]
                            if signed:
                                high = high * col_sign
                            rows = pl.ds(rr + q * N + par * H, RB)
                            put_l(0, rows, k, low + high)
                            put_l(1, rows, k, low - high)
            blocks(H // RB, body)

        def col_join(signed):
            def body(rr):
                for par in (0, 1):
                    for q in (0, 1):
                        rows = pl.ds(rr + q * N + par * H, RB)
                        for k in (0, 1):
                            even = rbuf[0, rows, pl.ds(k * H, H)]
                            odd = rbuf[1, rows, pl.ds(k * H, H)]
                            high = even - odd
                            if signed:
                                high = high * col_sign
                            put_d(par, rr, k, pl.ds(q * N, H), even + odd)
                            put_d(par, rr, k, pl.ds(q * N + H, H), high)
            blocks(H // RB, body)

        def roll_probe(step):
            for q in (0, 1):
                for k in (0, 1):
                    moved = pltpu.roll(probe[step, k], offsets[q][0], 0)
                    pw[q, k] = pltpu.roll(moved, offsets[q][1], 1)

        def forward_first(tbc, pump=lambda: None):
            def body(rr):
                for q in (0, 1):
                    r, c = offsets[q]
                    col_ok = col_index >= c
                    fields = []
                    for half in (0, 1):
                        rows = pl.ds(rr + half * H, RB)
                        row_ok = row_in_block + (rr + half * H) >= r
                        tr = window(tbc, 0, 0, rows, slice(None), row_ok, col_ok)
                        ti = window(tbc, 0, 1, rows, slice(None), row_ok, col_ok)
                        t0[q, 0, rows] = tr
                        t0[q, 1, rows] = ti
                        pr, pi = pw[q, 0, rows], pw[q, 1, rows]
                        fields.append((pr * tr - pi * ti, pr * ti + pi * tr))
                    for k in (0, 1):
                        high = fields[1][k] * row_sign
                        put_d(0, rr, k, pl.ds(q * N, N), fields[0][k] + high)
                        put_d(1, rr, k, pl.ds(q * N, N), fields[0][k] - high)
            blocks(H // RB, body)
            pump()
            left_product(0)
            pump()
            col_split(True)
            pump()
            right_product(1, psi)

        def forward_rest(tbc):
            def body(rr):
                for q in (0, 1):
                    r, c = offsets[q]
                    for par in (0, 1):
                        trows = pl.ds(rr + par * H, RB)
                        rows = pl.ds(rr + q * N + par * H, RB)
                        row_ok = 2 * (row_half + rr) + par >= r
                        for cp in (0, 1):
                            col_ok = 2 * col_half + cp >= c
                            cols = pl.ds(cp * H, H)
                            tr = window(tbc, 1, 0, trows, cols, row_ok, col_ok)
                            ti = window(tbc, 1, 1, trows, cols, row_ok, col_ok)
                            t1[q, 0, trows, cols] = tr
                            t1[q, 1, trows, cols] = ti
                            fr = psi[cp, rows, pl.ds(0, H)]
                            fi = psi[cp, rows, pl.ds(H, H)]
                            put_l(cp, rows, 0, fr * tr - fi * ti)
                            put_l(cp, rows, 1, fr * ti + fi * tr)
            blocks(H // RB, body)
            right_product(3, rbuf)
            col_join(False)
            left_product(2)

        def backward_first():
            def body(rr):
                for q in (0, 1):
                    cols = pl.ds(q * N, N)
                    er, ei = gbuf[0, pl.ds(rr, RB), cols], gbuf[0, pl.ds(rr + H, RB), cols]
                    odr, odi = gbuf[1, pl.ds(rr, RB), cols], gbuf[1, pl.ds(rr + H, RB), cols]
                    halves = []
                    for half, (fr, fi) in enumerate(((er + odr, ei + odi), (er - odr, ei - odi))):
                        m = meas[q, pl.ds(rr + half * H, RB)]
                        weight = 1.0 - m * lax.rsqrt(fr * fr + fi * fi + 1.0)
                        halves.append((weight * fr, weight * fi))
                    for k in (0, 1):
                        put_d(0, rr, k, cols, halves[0][k] + halves[1][k])
                        put_d(1, rr, k, cols, halves[0][k] - halves[1][k])
            blocks(H // RB, body)
            left_product(3)
            col_split(False)
            right_product(2, rbuf)

        def scatter(s, p, rows, cols, values, row_oks, col_oks):
            zero = jnp.zeros_like(values[0])
            upper = [jnp.where(row_oks[q], values[q], zero) for q in (0, 1)]
            lower = [values[q] - upper[q] for q in (0, 1)]
            for part, dst in ((upper, gor), (lower, gbc)):
                kept = [jnp.where(col_oks[q], part[q], zero) for q in (0, 1)]
                dst[0, s, p, rows, cols] = kept[0] + kept[1]
                dst[1, s, p, rows, cols] = (part[0] - kept[0]) + (part[1] - kept[1])

        def backward_second():
            def body(rr):
                for par in (0, 1):
                    trows = pl.ds(rr + par * H, RB)
                    row_oks = [2 * (row_half + rr) + par >= offsets[q][0] for q in (0, 1)]
                    for cp in (0, 1):
                        col_oks = [2 * col_half + cp >= offsets[q][1] for q in (0, 1)]
                        cols = pl.ds(cp * H, H)
                        grads = []
                        for q in (0, 1):
                            rows = pl.ds(rr + q * N + par * H, RB)
                            gr, gi = rbuf[cp, rows, pl.ds(0, H)], rbuf[cp, rows, pl.ds(H, H)]
                            fr, fi = psi[cp, rows, pl.ds(0, H)], psi[cp, rows, pl.ds(H, H)]
                            tr, ti = t1[q, 0, trows, cols], t1[q, 1, trows, cols]
                            grads.append((gr * fr + gi * fi, gi * fr - gr * fi))
                            put_l(cp, rows, 0, gr * tr + gi * ti)
                            put_l(cp, rows, 1, gi * tr - gr * ti)
                        for k in (0, 1):
                            scatter(1, k, trows, cols, [g[k] for g in grads], row_oks, col_oks)
            blocks(H // RB, body)

        def backward_last():
            right_product(0, rbuf)
            col_join(True)
            left_product(1)

            def body(rr):
                col_oks = [col_index >= offsets[q][1] for q in (0, 1)]
                for half in (0, 1):
                    rows = pl.ds(rr + half * H, RB)
                    row_oks = [row_in_block + (rr + half * H) >= offsets[q][0] for q in (0, 1)]
                    grads = []
                    for q in (0, 1):
                        cols = pl.ds(q * N, N)
                        er, ei = gbuf[0, pl.ds(rr, RB), cols], gbuf[0, pl.ds(rr + H, RB), cols]
                        odr, odi = gbuf[1, pl.ds(rr, RB), cols], gbuf[1, pl.ds(rr + H, RB), cols]
                        if half:
                            ur, ui = (er - odr) * row_sign, (ei - odi) * row_sign
                        else:
                            ur, ui = er + odr, ei + odi
                        pr, pi = pw[q, 0, rows], pw[q, 1, rows]
                        tr, ti = t0[q, 0, rows], t0[q, 1, rows]
                        grads.append((ur * pr + ui * pi, ui * pr - ur * pi))
                        gp[q, 0, rows] = ur * tr + ui * ti
                        gp[q, 1, rows] = ui * tr - ur * ti
                    for k in (0, 1):
                        scatter(0, k, rows, slice(None), [g[k] for g in grads], row_oks, col_oks)
            blocks(H // RB, body)

        def sum_probe():
            for k in (0, 1):
                parts = []
                for q in (0, 1):
                    back = pltpu.roll(gp[q, k], lax.rem(N - offsets[q][0], N), 0)
                    parts.append(pltpu.roll(back, lax.rem(N - offsets[q][1], N), 1))
                gsum[k] = parts[0] + parts[1]

        def reduction(step, ring):
            buf = step
            o0, o1, o2, o3, o4, o5, o6 = take(senders, 7)
            i0, i1, i2, i4, i5, i6 = take(arrivals, 6)
            i3 = take(arrivals, ny - 1 if ring else 1)
            c0 = remote(gsum.at[1 - core], r0.at[buf], mate, o0, i0)
            c1 = [remote(r0.at[buf, pl.ds(pl.multiple_of(lax.rem(x + d, nx) * xr, xr), xr)],
                         r1.at[buf, d - 1], xs[d - 1], o1, i1) for d in range(1, nx)]
            c2 = [remote(r1.at[buf, nx - 1, pl.ds(pl.multiple_of(lax.rem(z + d, nz) * zr, zr), zr)],
                         r2.at[buf, d - 1], zs[d - 1], o2, i2) for d in range(1, nz)]
            if ring:
                slots = [ry.at[buf, lax.rem(y + d, ny)] for d in range(ny - 1)]
                c3 = [remote(slot, slot, ys[-1], o3, i3[d]) for d, slot in enumerate(slots)]
            else:
                c3 = [remote(ry.at[buf, y], ry.at[buf, y], ys[d - 1], o3, i3[0]) for d in range(1, ny)]
            all_x, all_z = r1.at[buf, pl.ds(0, nx - 1)], r2.at[buf]
            all_y = ry.at[buf, pl.ds(0, ny - 1)]
            base_x = pl.multiple_of(x * xr, xr)
            base_z = pl.multiple_of(z * zr, zr)
            base = pl.multiple_of(x * xr + z * zr, zr)
            mine = probe.at[step + 1, core, pl.ds(base, zr)]
            strip = probe.at[step + 1, core, pl.ds(base_x, xr)]
            plane = probe.at[step + 1, core]
            c4 = [remote(mine, mine, zs[d - 1], o4, i4) for d in range(1, nz)]
            c5 = [remote(strip, strip, xs[d - 1], o5, i5) for d in range(1, nx)]
            c6 = remote(plane, plane, mate, o6, i6)

            def a0():
                c0.start()

            def a1():
                landed(r0.at[buf], i0)
                r0[buf] = r0[buf] + gsum[core]
                for c in c1:
                    c.start()

            def a2():
                total = r0[buf, pl.ds(base_x, xr)]
                landed(all_x, i1)
                for i in range(nx - 1):
                    total = total + r1[buf, i]
                r1[buf, nx - 1] = total
                for c in c2:
                    c.start()

            def a3():
                total = r1[buf, nx - 1, pl.ds(base_z, zr)]
                landed(all_z, i2)
                for i in range(nz - 1):
                    total = total + r2[buf, i]
                ry[buf, y] = total
                for c in c3[:1] if ring else c3:
                    c.start()

            def next_hop(i):
                landed(ry.at[buf, 0], i3[i - 1])
                c3[i].start()

            hops = [(lambda i=i: next_hop(i)) for i in range(1, ny - 1)] if ring else []

            def a4():
                landed(ry.at[buf, 0] if ring else all_y, i3[-1])
                total = ry[buf, 0]
                for i in range(1, ny):
                    total = total + ry[buf, i]
                scale = 0.5 / (n_ty * n_tx * 2)
                probe[step + 1, core, pl.ds(base, zr)] = probe[step, core, pl.ds(base, zr)] - scale * total
                for c in c4:
                    c.start()

            def a5():
                landed(all_z, i4)
                for c in c5:
                    c.start()

            def a6():
                landed(all_x, i5)
                c6.start()

            def a7():
                landed(r0.at[buf], i6)
                for ref, out in ((r0.at[buf], o0), (all_x, o1), (all_z, o2), (all_y, o3),
                                 (all_z, o4), (all_x, o5), (r0.at[buf], o6)):
                    gone(ref, out)

            return [a0, a1, a2, a3] + hops + [a4, a5, a6, a7]

        def add_above(part, place, step):
            s, p, rows = place
            gor[part, s, p, rows] = gor[part, s, p, rows] + has_above * ra[step, part, s, p, rows]

        def act(i):
            if i < len(actions):
                actions[i]()

        def follow(plan, steps):
            done = dict.fromkeys(steps, 0)
            for word in plan:
                for _ in range(int(word[1:] or 1)):
                    steps[word[0]](done[word[0]])
                    done[word[0]] += 1

        half = NCH // 2
        early = half + 2

        def relay(first, last):
            for i in range(first, last):
                s, p, rows = chunks(GATHER)[i]
                landed(tor.at[1, s, p, rows], in_right[i])
                right_up[i].start()

        relay(0, half)
        loads[2].wait()
        loads[3].wait()
        roll_probe(0)
        relay(half, early)
        landed(tbc1.at[0, 0], in_below[0])
        landed(tbc1.at[1, 0], in_corner[0])
        loads[4].wait()
        at = [early]

        def pump_gather():
            if at[0] < NCH:
                relay(at[0], at[0] + 1)
                at[0] += 1

        forward_first(tbc1, pump_gather)
        relay(at[0], NCH)
        landed(tbc1.at[0, 1], in_below[1])
        landed(tbc1.at[1, 1], in_corner[1])
        loads[5].wait()
        forward_rest(tbc1)
        backward_first()
        backward_second()
        gone(tor.at[0], out_left)
        gone(tor.at[0], out_up)
        gone(tor.at[1], out_right)

        places = chunks(MID)
        out_a, out_right, out_left, out_up = take(senders, 4)
        in_a, in_b, in_up = take(arrivals, NCH), take(arrivals, NCH), take(arrivals, 2)
        a_sends, b_right, b_left, c_up = [], [], [], []
        for i, (s, p, rows) in enumerate(places):
            a_sends.append([remote(gbc.at[part, s, p, rows], ra.at[0, part, s, p, rows], down, out_a, in_a[i])
                            for part in (0, 1)])
            b_right.append(remote(gor.at[1, s, p, rows], rb.at[0, s, p, rows], right, out_right, in_b[i]))
            b_left.append(remote(gor.at[0, s, p, rows], rb.at[1, s, p, rows], left, out_left, in_b[i]))
            c_up.append(remote(tor.at[:, s, p, rows], tbc2.at[:, s, p, rows], up, out_up, in_up[s]))
        for i in range(QUARTERS):
            for c in a_sends[i]:
                c.start()
        backward_last()
        sum_probe()
        actions = reduction(0, False)

        def mid_a(i):
            for c in a_sends[QUARTERS + i]:
                c.start()

        def mid_b(i):
            s, p, rows = places[i]
            landed(ra.at[0, :, s, p, rows], in_a[i])
            for part in (0, 1):
                add_above(part, places[i], 0)
            b_right[i].start()
            b_left[i].start()

        def mid_c(i):
            s, p, rows = places[i]
            landed(rb.at[:, s, p, rows], in_b[i])
            tor[0, s, p, rows] = tor[0, s, p, rows] - OBJ_STEP * (
                gor[0, s, p, rows] + has_left * rb[0, s, p, rows])
            tor[1, s, p, rows] = tor[1, s, p, rows] - OBJ_STEP * (
                gor[1, s, p, rows] + has_right * rb[1, s, p, rows])
            c_up[i].start()

        follow(MID_PLAN, dict(r=act, A=mid_a, B=mid_b, C=mid_c))
        roll_probe(1)
        landed(tbc2.at[:, 0], in_up[0])
        gone(gbc, out_a)

        at[0] = NCH - 2

        def pump_mid():
            if at[0] < NCH:
                mid_c(at[0])
                at[0] += 1

        forward_first(tbc2, pump_mid)
        gone(gor.at[1], out_right)
        gone(gor.at[0], out_left)
        landed(tbc2.at[:, 1], in_up[1])
        forward_rest(tbc2)
        backward_first()
        backward_second()
        gone(tor, out_up)
        places = chunks(LAST)
        out_a, out_right = take(senders, 2)
        in_a, in_b, in_below = take(arrivals, NCH), take(arrivals, NCH), take(arrivals, 4)
        a_sends, b_right = [], []
        for i, (s, p, rows) in enumerate(places):
            a_sends.append([remote(gbc.at[part, s, p, rows], ra.at[1, part, s, p, rows], down, out_a,
                                   in_a[i] if part else in_below[i // QUARTERS]) for part in (0, 1)])
            b_right.append(remote(gor.at[1, s, p, rows], rc.at[s, p, rows], right, out_right, in_b[i]))
        for i in range(half):
            a_sends[i][1].start()
        backward_last()
        sum_probe()
        actions = reduction(1, True)

        def end_b(i):
            s, p, rows = places[i]
            landed(ra.at[1, 1, s, p, rows], in_a[i])
            add_above(1, places[i], 1)
            b_right[i].start()

        def end_c(i):
            s, p, rows = places[i]
            if i % QUARTERS == 0:
                landed(ra.at[1, 0, s, p], in_below[i // QUARTERS])
            landed(rc.at[s, p, rows], in_b[i])
            value = tor[0, s, p, rows] - OBJ_STEP * (
                gor[0, s, p, rows] + has_above * ra[1, 0, s, p, rows] + has_left * rc[s, p, rows])
            if s == 0:
                result[0, p, rows] = value
            else:
                stage[p, rows] = value
            if i % QUARTERS == QUARTERS - 1:
                if s == 1:
                    result[1, p] = permute_cols(perm[0], permute_rows(perm[1], stage[p]))
                stores.append(pltpu.make_async_copy(result.at[s, p], obj_out.at[s, p], local.at[6 + len(stores)]))
                stores[-1].start()

        stores = []
        follow(END_PLAN, dict(r=act, K=lambda i: a_sends[half + i][1].start(),
                              L=lambda i: a_sends[i][0].start(), B=end_b, E=end_c))
        stores.append(pltpu.make_async_copy(probe.at[2], probe_out, local.at[10]))
        stores[-1].start()
        gone(gbc, out_a)
        gone(gor.at[1], out_right)
        for copy in stores:
            copy.wait()

    field = (2, 2, N, N)
    scratch = dict(
        tor=pltpu.VMEM((2,) + field, F32),
        tbc1=pltpu.VMEM((2,) + field, F32),
        tbc2=pltpu.VMEM((2,) + field, F32),
        gor=pltpu.VMEM((2,) + field, F32),
        gbc=pltpu.VMEM((2,) + field, F32),
        ra=pltpu.VMEM((2, 2) + field, F32),
        rb=pltpu.VMEM((2,) + field, F32),
        rc=pltpu.VMEM(field, F32),
        t0=pltpu.VMEM(field, F32),
        t1=pltpu.VMEM(field, F32),
        pw=pltpu.VMEM(field, F32),
        gp=pltpu.VMEM(field, F32),
        gsum=pltpu.VMEM((2, N, N), F32),
        probe=pltpu.VMEM((3, 2, N, N), F32),
        dhi=pltpu.VMEM((2, N, 2 * N), BF16),
        dlo=pltpu.VMEM((2, N, 2 * N), BF16),
        lhi=pltpu.VMEM((2, 2 * N, N), BF16),
        llo=pltpu.VMEM((2, 2 * N, N), BF16),
        gbuf=pltpu.VMEM((2, N, 2 * N), F32),
        rbuf=pltpu.VMEM((2, 2 * N, N), F32),
        psi=pltpu.VMEM((2, 2 * N, N), F32),
        meas=pltpu.VMEM((2, N, N), F32),
        mats=pltpu.VMEM((4, 2, 2, N, N), BF16),
        perm=pltpu.VMEM((2, N, N), BF16),
        stage=pltpu.VMEM((2, N, N), F32),
        result=pltpu.VMEM(field, F32),
        r0=pltpu.VMEM((2, N, N), F32),
        r1=pltpu.VMEM((2, nx, xr, N), F32),
        r2=pltpu.VMEM((2, nz - 1, zr, N), F32),
        ry=pltpu.VMEM((2, ny, zr, N), F32),
        send=pltpu.SemaphoreType.DMA((SENDERS,)),
        recv=pltpu.SemaphoreType.DMA((ARRIVALS,)),
        local=pltpu.SemaphoreType.DMA((11,)),
    )
    return kernel, list(scratch.values())


def publish(planes, probe):
    def kernel(planes_in, probe_in, planes_out, probe_out, sems):
        copies = [pltpu.make_async_copy(planes_in.at[s, p], planes_out.at[s, p], sems.at[2 * s + p])
                  for s in (0, 1) for p in (0, 1)]
        copies.append(pltpu.make_async_copy(probe_in, probe_out, sems.at[4]))
        for copy in copies:
            copy.start()
        for copy in copies:
            copy.wait()

    anywhere = pl.BlockSpec(memory_space=pl.ANY)
    return pl.pallas_call(
        kernel,
        out_shape=(jax.ShapeDtypeStruct(planes.shape, F32), jax.ShapeDtypeStruct(probe.shape, F32)),
        in_specs=[pl.BlockSpec(memory_space=pltpu.VMEM)] * 2,
        out_specs=(anywhere, anywhere),
        scratch_shapes=[pltpu.SemaphoreType.DMA((5,))],
    )(planes, probe)


def solution(mesh):
    n_ty, n_tx = mesh.shape["ty"], mesh.shape["tx"]
    kernel, scratch = make_kernel(n_ty, n_tx)
    mats, perm = tables(), shuffles()

    def body(object_planes, probe, positions, measured):
        found = pl.pallas_call(
            kernel,
            out_shape=(
                jax.ShapeDtypeStruct(object_planes.shape, F32),
                jax.ShapeDtypeStruct(probe.shape, F32),
            ),
            in_specs=[pl.BlockSpec(memory_space=pltpu.SMEM)] + [pl.BlockSpec(memory_space=pl.ANY)] * 5,
            out_specs=(pl.BlockSpec(memory_space=pl.ANY), pl.BlockSpec(memory_space=pl.ANY)),
            scratch_shapes=scratch,
            compiler_params=pltpu.CompilerParams(
                collective_id=0, has_side_effects=True, vmem_limit_bytes=56 * 1024 * 1024),
        )(positions, object_planes, probe, measured, jnp.asarray(mats), jnp.asarray(perm))
        return publish(*found)

    return jax.shard_map(
        body,
        mesh=mesh,
        in_specs=(
            P(None, None, "ty", "tx"),
            P(),
            P("ty", "tx", None, None),
            P("ty", "tx", None, None, None),
        ),
        out_specs=(P(None, None, "ty", "tx"), P()),
        check_vma=False,
    )
```

```python
import math

import jax
import jax.numpy as jnp
import numpy as np
from jax import lax
from jax.experimental import pallas as pl
from jax.experimental.pallas import tpu as pltpu
from jax.sharding import PartitionSpec as P
import ml_dtypes

MESH = pl.DeviceIdType.MESH
F32 = jnp.float32
BF16 = jnp.bfloat16
N = 256
H = 128
ITERS = 2
RB = 16
CR = 64
QUARTERS = N // CR
GATHER = [(0, 0), (0, 1), (1, 0), (1, 1)]
MID = [(1, 0), (0, 0), (0, 1), (1, 1)]
LAST = [(1, 0), (1, 1), (0, 0), (0, 1)]
NCH = 4 * QUARTERS
SENDERS = 24
ARRIVALS = 112
MID_PLAN = ("r", "A2", "r", "A4", "B2", "r", "A3", "B3", "r", "B3", "C3", "A3", "r", "B3", "C3", "r", "B3", "C3", "r", "B2", "C3", "r", "C2")
END_PLAN = ("r", "r", "B4", "r", "K8", "B4", "r", "L8", "B2", "r", "B3", "r", "B3", "r", "L8", "r", "E4", "r", "E4", "r", "E8")
OBJ_STEP = 0.1


def real_form(block):
    top = np.concatenate([block.real, -block.imag], axis=1)
    low = np.concatenate([block.imag, block.real], axis=1)
    return np.concatenate([top, low], axis=0)


def tables():
    k = np.arange(N)
    dft = np.exp(-2j * math.pi * ((k[:, None] * k[None, :]) % N) / N) / math.sqrt(N)
    chirp = np.exp(1j * math.pi * ((k * k) % (2 * N)) / N)
    prop = np.exp(-0.25j * math.pi) * chirp[:, None] * dft * chirp[None, :]
    kinds = []
    for kind in range(4):
        pars = []
        for par in (0, 1):
            if kind < 2:
                mat = real_form(prop[par::2, :H])
            else:
                mat = real_form(dft[:H, par::2])
            if kind % 2:
                mat = mat.T
            mat = mat.astype(np.float32)
            hi = mat.astype(ml_dtypes.bfloat16)
            lo = (mat - hi.astype(np.float32)).astype(ml_dtypes.bfloat16)
            pars.append(np.stack([hi, lo]))
        kinds.append(np.stack(pars))
    return np.stack(kinds)


def shuffles():
    perm = np.zeros((N, N), np.float32)
    j = np.arange(H)
    perm[j, 2 * j] = 1
    perm[H + j, 2 * j + 1] = 1
    return np.stack([perm, perm.T]).astype(ml_dtypes.bfloat16)


def split(x):
    hi = x.astype(BF16)
    return hi, (x - hi.astype(F32)).astype(BF16)


def split3(x):
    hi = x.astype(BF16)
    rest = x - hi.astype(F32)
    mid = rest.astype(BF16)
    return hi, mid, (rest - mid.astype(F32)).astype(BF16)


def dot(a, b):
    return jnp.dot(a, b, preferred_element_type=F32)


def permute_rows(perm, x):
    hi, mid, lo = split3(x)
    return dot(perm, hi) + dot(perm, mid) + dot(perm, lo)


def permute_cols(perm, x):
    hi, mid, lo = split3(x)
    return dot(hi, perm) + dot(mid, perm) + dot(lo, perm)


def blocks(count, body):
    def step(b, carry):
        body(pl.multiple_of(b * RB, RB))
        return carry

    lax.fori_loop(0, count, step, 0, unroll=True)


def make_kernel(n_ty, n_tx):
    ny = 4 if n_tx == 16 else 2
    nx = n_tx // ny
    nz = n_ty // 2
    xr = N // nx
    zr = xr // nz

    def kernel(pos, obj, probe_in, meas_in, mats_in, perm_in, obj_out, probe_out,
               tor, tbc1, tbc2, gor, gbc, ra, rb, rc, t0, t1, pw, gp, gsum, probe,
               dhi, dlo, lhi, llo, gbuf, rbuf, psi, meas, mats, perm, stage, result,
               r0, r1, r2, ry, send, recv, local):
        ty = lax.axis_index("ty")
        tx = lax.axis_index("tx")
        up = (lax.rem(ty + n_ty - 1, n_ty), tx)
        down = (lax.rem(ty + 1, n_ty), tx)
        left = (ty, lax.rem(tx + n_tx - 1, n_tx))
        right = (ty, lax.rem(tx + 1, n_tx))
        core = lax.rem(ty, 2)
        z = lax.div(ty, 2)
        x = lax.div(tx, ny)
        y = lax.rem(tx, ny)
        mate = (ty + 1 - 2 * core, tx)
        xs = [(ty, lax.rem(x + d, nx) * ny + y) for d in range(1, nx)]
        ys = [(ty, x * ny + lax.rem(y + d, ny)) for d in range(1, ny)]
        zs = [(lax.rem(z + d, nz) * 2 + core, tx) for d in range(1, nz)]
        has_above = jnp.where(ty > 0, 1.0, 0.0).astype(F32)
        has_below = jnp.where(ty < n_ty - 1, 1.0, 0.0).astype(F32)
        has_left = jnp.where(tx > 0, 1.0, 0.0).astype(F32)
        has_right = jnp.where(tx < n_tx - 1, 1.0, 0.0).astype(F32)

        senders, arrivals = iter(range(SENDERS)), iter(range(ARRIVALS))

        def remote(src, dst, device, out, into):
            return pltpu.make_async_remote_copy(
                src_ref=src, dst_ref=dst, send_sem=send.at[out], recv_sem=recv.at[into],
                device_id=device, device_id_type=MESH)

        def landed(ref, into):
            pltpu.make_async_copy(ref, ref, recv.at[into]).wait()

        def gone(ref, out):
            pltpu.make_async_copy(ref, ref, send.at[out]).wait()

        def take(source, count):
            return [next(source) for _ in range(count)]

        def chunks(order):
            return [(s, p, pl.ds(r * CR, CR)) for s, p in order for r in range(QUARTERS)]

        loads = [
            pltpu.make_async_copy(obj.at[1], stage, local.at[0]),
            pltpu.make_async_copy(perm_in, perm, local.at[1]),
            pltpu.make_async_copy(obj.at[0], tor.at[0, 0], local.at[2]),
            pltpu.make_async_copy(probe_in, probe.at[0], local.at[3]),
            pltpu.make_async_copy(mats_in, mats, local.at[4]),
            pltpu.make_async_copy(meas_in.at[0, 0], meas, local.at[5]),
        ]
        for copy in loads:
            copy.start()

        barrier = pltpu.get_barrier_semaphore()
        partners = [left, right, up, down] + xs + ys + zs
        for device in partners:
            pl.semaphore_signal(barrier, inc=1, device_id=device, device_id_type=MESH)
        pl.semaphore_wait(barrier, len(partners))

        own_left, own_up, right_up = [], [], []
        out_left, out_up, out_right = take(senders, 3)
        in_right, in_below, in_corner = take(arrivals, NCH), take(arrivals, 2), take(arrivals, 2)
        for i, (s, p, rows) in enumerate(chunks(GATHER)):
            src = obj.at[0, p, rows] if s == 0 else tor.at[0, 1, p, rows]
            own_left.append(remote(src, tor.at[1, s, p, rows], left, out_left, in_right[i]))
            own_up.append(remote(src, tbc1.at[0, s, p, rows], up, out_up, in_below[s]))
            right_up.append(remote(tor.at[1, s, p, rows], tbc1.at[1, s, p, rows], up, out_right, in_corner[s]))
        for i in range(NCH // 2):
            own_left[i].start()
            own_up[i].start()
        loads[0].wait()
        loads[1].wait()
        for p in (0, 1):
            tor[0, 1, p] = permute_cols(perm[1], permute_rows(perm[0], stage[p]))
            for i in range((2 + p) * QUARTERS, (3 + p) * QUARTERS):
                own_left[i].start()
                own_up[i].start()

        row_in_block = lax.broadcasted_iota(jnp.int32, (RB, N), 0)
        col_index = lax.broadcasted_iota(jnp.int32, (RB, N), 1)
        col_half = lax.broadcasted_iota(jnp.int32, (RB, H), 1)
        row_half = lax.broadcasted_iota(jnp.int32, (RB, H), 0)
        row_sign = jnp.where(lax.rem(row_in_block, 2) == 1, -1.0, 1.0).astype(F32)
        col_sign = jnp.where(lax.rem(col_half, 2) == 1, -1.0, 1.0).astype(F32)
        offsets = [(pos[0, 0, 0, 0], pos[0, 0, 0, 1]), (pos[0, 0, 1, 0], pos[0, 0, 1, 1])]

        def window(tbc, s, p, rows, cols, row_ok, col_ok):
            upper = jnp.where(col_ok, tor[0, s, p, rows, cols], has_right * tor[1, s, p, rows, cols])
            lower = jnp.where(col_ok, tbc[0, s, p, rows, cols], has_right * tbc[1, s, p, rows, cols])
            return jnp.where(row_ok, upper, has_below * lower)

        def put_d(par, rr, k, cols, value):
            hi, lo = split(value)
            rows = pl.ds(rr + k * H, RB)
            dhi[par, rows, cols] = hi
            dlo[par, rows, cols] = lo

        def put_l(cp, rows, k, value):
            hi, lo = split(value)
            cols = pl.ds(k * H, H)
            lhi[cp, rows, cols] = hi
            llo[cp, rows, cols] = lo

        def left_product(kind):
            for par in (0, 1):
                a_hi, a_lo = mats[kind, par, 0], mats[kind, par, 1]
                gbuf[par] = dot(a_lo, dhi[par]) + dot(a_hi, dlo[par]) + dot(a_hi, dhi[par])

        def right_product(kind, out):
            for cp in (0, 1):
                b_hi, b_lo = mats[kind, cp, 0], mats[kind, cp, 1]
                out[cp] = dot(lhi[cp], b_lo) + dot(llo[cp], b_hi) + dot(lhi[cp], b_hi)

        def col_split(signed):
            def body(rr):
                for par in (0, 1):
                    for q in (0, 1):
                        for k in (0, 1):
                            low = gbuf[par, pl.ds(rr + k * H, RB), pl.ds(q * N, H)]
                            high = gbuf[par, pl.ds(rr + k * H, RB), pl.ds(q * N + H, H)]
                            if signed:
                                high = high * col_sign
                            rows = pl.ds(rr + q * N + par * H, RB)
                            put_l(0, rows, k, low + high)
                            put_l(1, rows, k, low - high)
            blocks(H // RB, body)

        def col_join(signed):
            def body(rr):
                for par in (0, 1):
                    for q in (0, 1):
                        rows = pl.ds(rr + q * N + par * H, RB)
                        for k in (0, 1):
                            even = rbuf[0, rows, pl.ds(k * H, H)]
                            odd = rbuf[1, rows, pl.ds(k * H, H)]
                            high = even - odd
                            if signed:
                                high = high * col_sign
                            put_d(par, rr, k, pl.ds(q * N, H), even + odd)
                            put_d(par, rr, k, pl.ds(q * N + H, H), high)
            blocks(H // RB, body)

        def roll_probe(step):
            for q in (0, 1):
                for k in (0, 1):
                    moved = pltpu.roll(probe[step, k], offsets[q][0], 0)
                    pw[q, k] = pltpu.roll(moved, offsets[q][1], 1)

        def forward_first(tbc, pump=lambda: None):
            def body(rr):
                for q in (0, 1):
                    r, c = offsets[q]
                    col_ok = col_index >= c
                    fields = []
                    for half in (0, 1):
                        rows = pl.ds(rr + half * H, RB)
                        row_ok = row_in_block + (rr + half * H) >= r
                        tr = window(tbc, 0, 0, rows, slice(None), row_ok, col_ok)
                        ti = window(tbc, 0, 1, rows, slice(None), row_ok, col_ok)
                        t0[q, 0, rows] = tr
                        t0[q, 1, rows] = ti
                        pr, pi = pw[q, 0, rows], pw[q, 1, rows]
                        fields.append((pr * tr - pi * ti, pr * ti + pi * tr))
                    for k in (0, 1):
                        high = fields[1][k] * row_sign
                        put_d(0, rr, k, pl.ds(q * N, N), fields[0][k] + high)
                        put_d(1, rr, k, pl.ds(q * N, N), fields[0][k] - high)
            blocks(H // RB, body)
            pump()
            left_product(0)
            pump()
            col_split(True)
            pump()
            right_product(1, psi)

        def forward_rest(tbc):
            def body(rr):
                for q in (0, 1):
                    r, c = offsets[q]
                    for par in (0, 1):
                        trows = pl.ds(rr + par * H, RB)
                        rows = pl.ds(rr + q * N + par * H, RB)
                        row_ok = 2 * (row_half + rr) + par >= r
                        for cp in (0, 1):
                            col_ok = 2 * col_half + cp >= c
                            cols = pl.ds(cp * H, H)
                            tr = window(tbc, 1, 0, trows, cols, row_ok, col_ok)
                            ti = window(tbc, 1, 1, trows, cols, row_ok, col_ok)
                            t1[q, 0, trows, cols] = tr
                            t1[q, 1, trows, cols] = ti
                            fr = psi[cp, rows, pl.ds(0, H)]
                            fi = psi[cp, rows, pl.ds(H, H)]
                            put_l(cp, rows, 0, fr * tr - fi * ti)
                            put_l(cp, rows, 1, fr * ti + fi * tr)
            blocks(H // RB, body)
            right_product(3, rbuf)
            col_join(False)
            left_product(2)

        def backward_first():
            def body(rr):
                for q in (0, 1):
                    cols = pl.ds(q * N, N)
                    er, ei = gbuf[0, pl.ds(rr, RB), cols], gbuf[0, pl.ds(rr + H, RB), cols]
                    odr, odi = gbuf[1, pl.ds(rr, RB), cols], gbuf[1, pl.ds(rr + H, RB), cols]
                    halves = []
                    for half, (fr, fi) in enumerate(((er + odr, ei + odi), (er - odr, ei - odi))):
                        m = meas[q, pl.ds(rr + half * H, RB)]
                        weight = 1.0 - m * lax.rsqrt(fr * fr + fi * fi + 1.0)
                        halves.append((weight * fr, weight * fi))
                    for k in (0, 1):
                        put_d(0, rr, k, cols, halves[0][k] + halves[1][k])
                        put_d(1, rr, k, cols, halves[0][k] - halves[1][k])
            blocks(H // RB, body)
            left_product(3)
            col_split(False)
            right_product(2, rbuf)

        def scatter(s, p, rows, cols, values, row_oks, col_oks):
            zero = jnp.zeros_like(values[0])
            upper = [jnp.where(row_oks[q], values[q], zero) for q in (0, 1)]
            lower = [values[q] - upper[q] for q in (0, 1)]
            for part, dst in ((upper, gor), (lower, gbc)):
                kept = [jnp.where(col_oks[q], part[q], zero) for q in (0, 1)]
                dst[0, s, p, rows, cols] = kept[0] + kept[1]
                dst[1, s, p, rows, cols] = (part[0] - kept[0]) + (part[1] - kept[1])

        def backward_second():
            def body(rr):
                for par in (0, 1):
                    trows = pl.ds(rr + par * H, RB)
                    row_oks = [2 * (row_half + rr) + par >= offsets[q][0] for q in (0, 1)]
                    for cp in (0, 1):
                        col_oks = [2 * col_half + cp >= offsets[q][1] for q in (0, 1)]
                        cols = pl.ds(cp * H, H)
                        grads = []
                        for q in (0, 1):
                            rows = pl.ds(rr + q * N + par * H, RB)
                            gr, gi = rbuf[cp, rows, pl.ds(0, H)], rbuf[cp, rows, pl.ds(H, H)]
                            fr, fi = psi[cp, rows, pl.ds(0, H)], psi[cp, rows, pl.ds(H, H)]
                            tr, ti = t1[q, 0, trows, cols], t1[q, 1, trows, cols]
                            grads.append((gr * fr + gi * fi, gi * fr - gr * fi))
                            put_l(cp, rows, 0, gr * tr + gi * ti)
                            put_l(cp, rows, 1, gi * tr - gr * ti)
                        for k in (0, 1):
                            scatter(1, k, trows, cols, [g[k] for g in grads], row_oks, col_oks)
            blocks(H // RB, body)

        def backward_last():
            right_product(0, rbuf)
            col_join(True)
            left_product(1)

            def body(rr):
                col_oks = [col_index >= offsets[q][1] for q in (0, 1)]
                for half in (0, 1):
                    rows = pl.ds(rr + half * H, RB)
                    row_oks = [row_in_block + (rr + half * H) >= offsets[q][0] for q in (0, 1)]
                    grads = []
                    for q in (0, 1):
                        cols = pl.ds(q * N, N)
                        er, ei = gbuf[0, pl.ds(rr, RB), cols], gbuf[0, pl.ds(rr + H, RB), cols]
                        odr, odi = gbuf[1, pl.ds(rr, RB), cols], gbuf[1, pl.ds(rr + H, RB), cols]
                        if half:
                            ur, ui = (er - odr) * row_sign, (ei - odi) * row_sign
                        else:
                            ur, ui = er + odr, ei + odi
                        pr, pi = pw[q, 0, rows], pw[q, 1, rows]
                        tr, ti = t0[q, 0, rows], t0[q, 1, rows]
                        grads.append((ur * pr + ui * pi, ui * pr - ur * pi))
                        gp[q, 0, rows] = ur * tr + ui * ti
                        gp[q, 1, rows] = ui * tr - ur * ti
                    for k in (0, 1):
                        scatter(0, k, rows, slice(None), [g[k] for g in grads], row_oks, col_oks)
            blocks(H // RB, body)

        def sum_probe():
            for k in (0, 1):
                parts = []
                for q in (0, 1):
                    back = pltpu.roll(gp[q, k], lax.rem(N - offsets[q][0], N), 0)
                    parts.append(pltpu.roll(back, lax.rem(N - offsets[q][1], N), 1))
                gsum[k] = parts[0] + parts[1]

        def reduction(step, ring):
            buf = step
            o0, o1, o2, o3, o4, o5, o6 = take(senders, 7)
            i0, i1, i2, i4, i5, i6 = take(arrivals, 6)
            i3 = take(arrivals, ny - 1 if ring else 1)
            c0 = remote(gsum.at[1 - core], r0.at[buf], mate, o0, i0)
            c1 = [remote(r0.at[buf, pl.ds(pl.multiple_of(lax.rem(x + d, nx) * xr, xr), xr)],
                         r1.at[buf, d - 1], xs[d - 1], o1, i1) for d in range(1, nx)]
            c2 = [remote(r1.at[buf, nx - 1, pl.ds(pl.multiple_of(lax.rem(z + d, nz) * zr, zr), zr)],
                         r2.at[buf, d - 1], zs[d - 1], o2, i2) for d in range(1, nz)]
            if ring:
                slots = [ry.at[buf, lax.rem(y + d, ny)] for d in range(ny - 1)]
                c3 = [remote(slot, slot, ys[-1], o3, i3[d]) for d, slot in enumerate(slots)]
            else:
                c3 = [remote(ry.at[buf, y], ry.at[buf, y], ys[d - 1], o3, i3[0]) for d in range(1, ny)]
            all_x, all_z = r1.at[buf, pl.ds(0, nx - 1)], r2.at[buf]
            all_y = ry.at[buf, pl.ds(0, ny - 1)]
            base_x = pl.multiple_of(x * xr, xr)
            base_z = pl.multiple_of(z * zr, zr)
            base = pl.multiple_of(x * xr + z * zr, zr)
            mine = probe.at[step + 1, core, pl.ds(base, zr)]
            strip = probe.at[step + 1, core, pl.ds(base_x, xr)]
            plane = probe.at[step + 1, core]
            c4 = [remote(mine, mine, zs[d - 1], o4, i4) for d in range(1, nz)]
            c5 = [remote(strip, strip, xs[d - 1], o5, i5) for d in range(1, nx)]
            c6 = remote(plane, plane, mate, o6, i6)

            def a0():
                c0.start()

            def a1():
                landed(r0.at[buf], i0)
                r0[buf] = r0[buf] + gsum[core]
                for c in c1:
                    c.start()

            def a2():
                total = r0[buf, pl.ds(base_x, xr)]
                landed(all_x, i1)
                for i in range(nx - 1):
                    total = total + r1[buf, i]
                r1[buf, nx - 1] = total
                for c in c2:
                    c.start()

            def a3():
                total = r1[buf, nx - 1, pl.ds(base_z, zr)]
                landed(all_z, i2)
                for i in range(nz - 1):
                    total = total + r2[buf, i]
                ry[buf, y] = total
                for c in c3[:1] if ring else c3:
                    c.start()

            def next_hop(i):
                landed(ry.at[buf, 0], i3[i - 1])
                c3[i].start()

            hops = [(lambda i=i: next_hop(i)) for i in range(1, ny - 1)] if ring else []

            def a4():
                landed(ry.at[buf, 0] if ring else all_y, i3[-1])
                total = ry[buf, 0]
                for i in range(1, ny):
                    total = total + ry[buf, i]
                scale = 0.5 / (n_ty * n_tx * 2)
                probe[step + 1, core, pl.ds(base, zr)] = probe[step, core, pl.ds(base, zr)] - scale * total
                for c in c4:
                    c.start()

            def a5():
                landed(all_z, i4)
                for c in c5:
                    c.start()

            def a6():
                landed(all_x, i5)
                c6.start()

            def a7():
                landed(r0.at[buf], i6)
                for ref, out in ((r0.at[buf], o0), (all_x, o1), (all_z, o2), (all_y, o3),
                                 (all_z, o4), (all_x, o5), (r0.at[buf], o6)):
                    gone(ref, out)

            return [a0, a1, a2, a3] + hops + [a4, a5, a6, a7]

        def add_above(part, place, step):
            s, p, rows = place
            gor[part, s, p, rows] = gor[part, s, p, rows] + has_above * ra[step, part, s, p, rows]

        def act(i):
            if i < len(actions):
                actions[i]()

        def follow(plan, steps):
            done = dict.fromkeys(steps, 0)
            for word in plan:
                for _ in range(int(word[1:] or 1)):
                    steps[word[0]](done[word[0]])
                    done[word[0]] += 1

        half = NCH // 2
        early = half + 2

        def relay(first, last):
            for i in range(first, last):
                s, p, rows = chunks(GATHER)[i]
                landed(tor.at[1, s, p, rows], in_right[i])
                right_up[i].start()

        relay(0, half)
        loads[2].wait()
        loads[3].wait()
        roll_probe(0)
        relay(half, early)
        landed(tbc1.at[0, 0], in_below[0])
        landed(tbc1.at[1, 0], in_corner[0])
        loads[4].wait()
        at = [early]

        def pump_gather():
            if at[0] < NCH:
                relay(at[0], at[0] + 1)
                at[0] += 1

        forward_first(tbc1, pump_gather)
        relay(at[0], NCH)
        landed(tbc1.at[0, 1], in_below[1])
        landed(tbc1.at[1, 1], in_corner[1])
        loads[5].wait()
        forward_rest(tbc1)
        backward_first()
        backward_second()
        gone(tor.at[0], out_left)
        gone(tor.at[0], out_up)
        gone(tor.at[1], out_right)

        places = chunks(MID)
        out_a, out_right, out_left, out_up = take(senders, 4)
        in_a, in_b, in_up = take(arrivals, NCH), take(arrivals, NCH), take(arrivals, 2)
        a_sends, b_right, b_left, c_up = [], [], [], []
        for i, (s, p, rows) in enumerate(places):
            a_sends.append([remote(gbc.at[part, s, p, rows], ra.at[0, part, s, p, rows], down, out_a, in_a[i])
                            for part in (0, 1)])
            b_right.append(remote(gor.at[1, s, p, rows], rb.at[0, s, p, rows], right, out_right, in_b[i]))
            b_left.append(remote(gor.at[0, s, p, rows], rb.at[1, s, p, rows], left, out_left, in_b[i]))
            c_up.append(remote(tor.at[:, s, p, rows], tbc2.at[:, s, p, rows], up, out_up, in_up[s]))
        for i in range(QUARTERS):
            for c in a_sends[i]:
                c.start()
        backward_last()
        sum_probe()
        actions = reduction(0, False)

        def mid_a(i):
            for c in a_sends[QUARTERS + i]:
                c.start()

        def mid_b(i):
            s, p, rows = places[i]
            landed(ra.at[0, :, s, p, rows], in_a[i])
            for part in (0, 1):
                add_above(part, places[i], 0)
            b_right[i].start()
            b_left[i].start()

        def mid_c(i):
            s, p, rows = places[i]
            landed(rb.at[:, s, p, rows], in_b[i])
            tor[0, s, p, rows] = tor[0, s, p, rows] - OBJ_STEP * (
                gor[0, s, p, rows] + has_left * rb[0, s, p, rows])
            tor[1, s, p, rows] = tor[1, s, p, rows] - OBJ_STEP * (
                gor[1, s, p, rows] + has_right * rb[1, s, p, rows])
            c_up[i].start()

        follow(MID_PLAN, dict(r=act, A=mid_a, B=mid_b, C=mid_c))
        roll_probe(1)
        landed(tbc2.at[:, 0], in_up[0])
        gone(gbc, out_a)

        at[0] = NCH - 2

        def pump_mid():
            if at[0] < NCH:
                mid_c(at[0])
                at[0] += 1

        forward_first(tbc2, pump_mid)
        gone(gor.at[1], out_right)
        gone(gor.at[0], out_left)
        landed(tbc2.at[:, 1], in_up[1])
        forward_rest(tbc2)
        backward_first()
        backward_second()
        gone(tor, out_up)
        places = chunks(LAST)
        out_a, out_right = take(senders, 2)
        in_a, in_b, in_below = take(arrivals, NCH), take(arrivals, NCH), take(arrivals, 4)
        a_sends, b_right = [], []
        for i, (s, p, rows) in enumerate(places):
            a_sends.append([remote(gbc.at[part, s, p, rows], ra.at[1, part, s, p, rows], down, out_a,
                                   in_a[i] if part else in_below[i // QUARTERS]) for part in (0, 1)])
            b_right.append(remote(gor.at[1, s, p, rows], rc.at[s, p, rows], right, out_right, in_b[i]))
        for i in range(half):
            a_sends[i][1].start()
        backward_last()
        sum_probe()
        actions = reduction(1, True)

        def end_b(i):
            s, p, rows = places[i]
            landed(ra.at[1, 1, s, p, rows], in_a[i])
            add_above(1, places[i], 1)
            b_right[i].start()

        def end_c(i):
            s, p, rows = places[i]
            if i % QUARTERS == 0:
                landed(ra.at[1, 0, s, p], in_below[i // QUARTERS])
            landed(rc.at[s, p, rows], in_b[i])
            value = tor[0, s, p, rows] - OBJ_STEP * (
                gor[0, s, p, rows] + has_above * ra[1, 0, s, p, rows] + has_left * rc[s, p, rows])
            if s == 0:
                result[0, p, rows] = value
            else:
                stage[p, rows] = value
            if i % QUARTERS == QUARTERS - 1:
                if s == 1:
                    result[1, p] = permute_cols(perm[0], permute_rows(perm[1], stage[p]))
                stores.append(pltpu.make_async_copy(result.at[s, p], obj_out.at[s, p], local.at[6 + len(stores)]))
                stores[-1].start()

        stores = []
        follow(END_PLAN, dict(r=act, K=lambda i: a_sends[half + i][1].start(),
                              L=lambda i: a_sends[i][0].start(), B=end_b, E=end_c))
        stores.append(pltpu.make_async_copy(probe.at[2], probe_out, local.at[10]))
        stores[-1].start()
        gone(gbc, out_a)
        gone(gor.at[1], out_right)
        for copy in stores:
            copy.wait()

    field = (2, 2, N, N)
    scratch = dict(
        tor=pltpu.VMEM((2,) + field, F32),
        tbc1=pltpu.VMEM((2,) + field, F32),
        tbc2=pltpu.VMEM((2,) + field, F32),
        gor=pltpu.VMEM((2,) + field, F32),
        gbc=pltpu.VMEM((2,) + field, F32),
        ra=pltpu.VMEM((2, 2) + field, F32),
        rb=pltpu.VMEM((2,) + field, F32),
        rc=pltpu.VMEM(field, F32),
        t0=pltpu.VMEM(field, F32),
        t1=pltpu.VMEM(field, F32),
        pw=pltpu.VMEM(field, F32),
        gp=pltpu.VMEM(field, F32),
        gsum=pltpu.VMEM((2, N, N), F32),
        probe=pltpu.VMEM((3, 2, N, N), F32),
        dhi=pltpu.VMEM((2, N, 2 * N), BF16),
        dlo=pltpu.VMEM((2, N, 2 * N), BF16),
        lhi=pltpu.VMEM((2, 2 * N, N), BF16),
        llo=pltpu.VMEM((2, 2 * N, N), BF16),
        gbuf=pltpu.VMEM((2, N, 2 * N), F32),
        rbuf=pltpu.VMEM((2, 2 * N, N), F32),
        psi=pltpu.VMEM((2, 2 * N, N), F32),
        meas=pltpu.VMEM((2, N, N), F32),
        mats=pltpu.VMEM((4, 2, 2, N, N), BF16),
        perm=pltpu.VMEM((2, N, N), BF16),
        stage=pltpu.VMEM((2, N, N), F32),
        result=pltpu.VMEM(field, F32),
        r0=pltpu.VMEM((2, N, N), F32),
        r1=pltpu.VMEM((2, nx, xr, N), F32),
        r2=pltpu.VMEM((2, nz - 1, zr, N), F32),
        ry=pltpu.VMEM((2, ny, zr, N), F32),
        send=pltpu.SemaphoreType.DMA((SENDERS,)),
        recv=pltpu.SemaphoreType.DMA((ARRIVALS,)),
        local=pltpu.SemaphoreType.DMA((11,)),
    )
    return kernel, list(scratch.values())


def publish(planes, probe):
    def kernel(planes_in, probe_in, planes_out, probe_out, sems):
        copies = [pltpu.make_async_copy(planes_in.at[s, p], planes_out.at[s, p], sems.at[2 * s + p])
                  for s in (0, 1) for p in (0, 1)]
        copies.append(pltpu.make_async_copy(probe_in, probe_out, sems.at[4]))
        for copy in copies:
            copy.start()
        for copy in copies:
            copy.wait()

    anywhere = pl.BlockSpec(memory_space=pl.ANY)
    return pl.pallas_call(
        kernel,
        out_shape=(jax.ShapeDtypeStruct(planes.shape, F32), jax.ShapeDtypeStruct(probe.shape, F32)),
        in_specs=[pl.BlockSpec(memory_space=pltpu.VMEM)] * 2,
        out_specs=(anywhere, anywhere),
        scratch_shapes=[pltpu.SemaphoreType.DMA((5,))],
    )(planes, probe)


def solution(mesh):
    n_ty, n_tx = mesh.shape["ty"], mesh.shape["tx"]
    kernel, scratch = make_kernel(n_ty, n_tx)
    mats, perm = tables(), shuffles()

    def body(object_planes, probe, positions, measured):
        found = pl.pallas_call(
            kernel,
            out_shape=(
                jax.ShapeDtypeStruct(object_planes.shape, F32),
                jax.ShapeDtypeStruct(probe.shape, F32),
            ),
            in_specs=[pl.BlockSpec(memory_space=pltpu.SMEM)] + [pl.BlockSpec(memory_space=pl.ANY)] * 5,
            out_specs=(pl.BlockSpec(memory_space=pl.ANY), pl.BlockSpec(memory_space=pl.ANY)),
            scratch_shapes=scratch,
            compiler_params=pltpu.CompilerParams(
                collective_id=0, has_side_effects=True, vmem_limit_bytes=56 * 1024 * 1024),
        )(positions, object_planes, probe, measured, jnp.asarray(mats), jnp.asarray(perm))
        return publish(*found)

    return jax.shard_map(
        body,
        mesh=mesh,
        in_specs=(
            P(None, None, "ty", "tx"),
            P(),
            P("ty", "tx", None, None),
            P("ty", "tx", None, None, None),
        ),
        out_specs=(P(None, None, "ty", "tx"), P()),
        check_vma=False,
    )
```
